32 devices in a mesh: dp: 2 (over y), ctx: 4 (over z), tp: 4 (over x, core).
Axes of the slice: x: 2, y: 2, z: 4, core: 2. Of those that a mesh axis runs over, the one named last changes fastest.
Arguments:
- tokens: bfloat16 [4, 1024, 1024], P('dp', ('ctx', 'tp')), may hold values from -6 to 6
- segments: int32 [4, 1024], P('dp'), may hold values from 0 to 2, as said below
- ln1_gain: float32 [1024], replicated, may hold values from 0.25 to 1.75
- ln1_bias: float32 [1024], replicated, may hold values from -4 to 4
- qkv_weight: bfloat16 [1024, 3, 1024], P('dp', None, 'tp'), may hold values from -0.1875 to 0.1875
- qkv_bias: float32 [3, 1024], P(None, 'tp'), may hold values from -4 to 4
- out_weight: bfloat16 [1024, 1024], P('tp', 'dp'), may hold values from -1.5 to 1.5
- out_bias: float32 [1024], replicated, may hold values from -4 to 4
- ln2_gain: float32 [1024], replicated, may hold values from 0.25 to 1.75
- ln2_bias: float32 [1024], replicated, may hold values from -4 to 4
- fc_weight: bfloat16 [1024, 4096], P('dp', 'tp'), may hold values from -0.1875 to 0.1875
- fc_bias: float32 [4096], P('tp'), may hold values from -4 to 4
- proj_weight: bfloat16 [4096, 1024], P('tp', 'dp'), may hold values from -0.09375 to 0.09375
- proj_bias: float32 [1024], replicated, may hold values from -4 to 4
- grad_out: bfloat16 [4, 1024, 1024], P('dp', ('ctx', 'tp')), may hold values from -6 to 6
Outputs:
- block_out: bfloat16 [4, 1024, 1024], P('dp', ('ctx', 'tp'))
- tokens_grad: float32 [4, 1024, 1024], P('dp', ('ctx', 'tp'))
- ln1_gain_grad: float32 [1024], replicated
- ln1_bias_grad: float32 [1024], replicated
- qkv_weight_grad: float32 [1024, 3, 1024], P('dp', None, 'tp')
- qkv_bias_grad: float32 [3, 1024], P(None, 'tp')
- out_weight_grad: float32 [1024, 1024], P('tp', 'dp')
- out_bias_grad: float32 [1024], replicated
- ln2_gain_grad: float32 [1024], replicated
- ln2_bias_grad: float32 [1024], replicated
- fc_weight_grad: float32 [1024, 4096], P('dp', 'tp')
- fc_bias_grad: float32 [4096], P('tp')
- proj_weight_grad: float32 [4096, 1024], P('tp', 'dp')
- proj_bias_grad: float32 [1024], replicated
The draws below stay inside these ranges and needn't reach their ends.
Inputs may be any that keep to these rules, and one draw needn't show every extreme that they name: `segments`: segment numbers never fall along a sequence, and each of 0, 1 and 2 occurs in every sequence.
All inputs are finite; a program needn't handle non-finite values.
Results may differ from the reference program's by a relative error of at most 0.012.
The reference program's roundings to bfloat16 on the way count: a program that leaves them out, or rounds other values in their place, can miss the bound.
Values may be sent and summed in bfloat16 or wider, within the bound.
A program may use at most 128 MiB of HBM per device.

```python
import jax
import jax.numpy as jnp
from jax import lax

D = 1024
H = 16
HD = 64
FF = 4096
SEQ_LEN = 1024
SEQS = 4


def draw_segments(key, part):
    key = jax.random.fold_in(key, 11)
    first_key, last_key = jax.random.split(key)
    opening = jax.random.randint(first_key, (SEQS, 1), SEQ_LEN // 5, SEQ_LEN // 4)
    closing = SEQ_LEN - jax.random.randint(last_key, (SEQS, 1), SEQ_LEN // 5, SEQ_LEN // 4)
    position = jnp.arange(SEQ_LEN, dtype=jnp.int32)[None, :]
    return (position >= opening).astype(jnp.int32) + (position >= closing).astype(jnp.int32)


def raised(drawn, key, source, target, shards_of, factor):
    def block_of(dim):
        return (jnp.arange(drawn.shape[dim]) // (drawn.shape[dim] // shards_of)).reshape((-1,) + (1,) * (drawn.ndim - 1 - dim))

    one_side = jax.random.permutation(key, shards_of)[block_of(target)]
    other_side = (block_of(target) + shards_of // 2) % shards_of
    return jnp.where((block_of(source) == one_side) | (block_of(source) == other_side), factor * drawn, drawn)


def level_of(key, dims, pieces, least, high):
    level = 1.0
    for dim, shards_of in pieces:
        heights = jax.random.uniform(jax.random.fold_in(jax.random.fold_in(key, 6), dim), (shards_of,), jnp.float32, least / len(pieces), high / len(pieces))
        level = level * jnp.repeat(jnp.exp(heights), dims[dim] // shards_of).reshape((-1,) + (1,) * (len(dims) - 1 - dim))
    return level


def centred(stream_key, shape, deviation, bound, pieces=(), kind=jnp.bfloat16):
    drawn = deviation * jax.random.normal(stream_key, shape, jnp.float32)
    if pieces:
        drawn = drawn * level_of(stream_key, shape, pieces, -0.22, 0.18)
    return jnp.clip(drawn, -bound, bound).astype(kind)


def heavy_noise(stream_key, extent, scale, most, cuts, heavy, held_as=jnp.bfloat16):
    entries = scale * jax.random.normal(stream_key, extent, jnp.float32)
    if cuts:
        entries = entries * level_of(stream_key, extent, cuts, -0.22, 0.18)
    return jnp.clip(raised(entries, jax.random.fold_in(stream_key, 3), *heavy), -most, most).astype(held_as)


def setup_inputs(seed: int = 0) -> dict:
    arg_keys = jax.random.split(jax.random.key(seed), 16)
    return {
        "tokens": heavy_noise(arg_keys[0], (SEQS, SEQ_LEN, D), 1.0, 6.0, ((0, 2), (1, 16)), (0, 2, 2, 2.0)),
        "segments": draw_segments(jax.random.fold_in(arg_keys[15], 71), 0),
        "ln1_gain": jnp.clip(1.0 + 0.15 * jax.random.normal(arg_keys[2], (D,), jnp.float32), 0.25, 1.75),
        "ln1_bias": centred(arg_keys[3], (D,), 0.3, 4.0, (), jnp.float32),
        "qkv_weight": centred(arg_keys[4], (D, 3, D), D ** -0.5, 0.1875, ((0, 2), (2, 4))),
        "qkv_bias": centred(arg_keys[5], (3, D), 0.3, 4.0, ((1, 4),), jnp.float32),
        "out_weight": centred(arg_keys[6], (D, D), (D // 64) ** -0.5, 1.5, ((0, 4), (1, 2))),
        "out_bias": centred(arg_keys[7], (D,), 0.3, 4.0, (), jnp.float32),
        "ln2_gain": jnp.clip(1.0 + 0.15 * jax.random.normal(arg_keys[8], (D,), jnp.float32), 0.25, 1.75),
        "ln2_bias": centred(arg_keys[9], (D,), 0.3, 4.0, (), jnp.float32),
        "fc_weight": centred(arg_keys[10], (D, FF), D ** -0.5, 0.1875, ((0, 2), (1, 4))),
        "fc_bias": centred(arg_keys[11], (FF,), 0.3, 4.0, ((0, 4),), jnp.float32),
        "proj_weight": centred(arg_keys[12], (FF, D), FF ** -0.5, 0.09375, ((0, 4), (1, 2))),
        "proj_bias": centred(arg_keys[13], (D,), 0.3, 4.0, (), jnp.float32),
        "grad_out": heavy_noise(arg_keys[14], (SEQS, SEQ_LEN, D), 1.0, 6.0, ((0, 2), (1, 16)), (0, 2, 2, 2.0)),
    }


@jax.custom_vjp
def low(v):
    return lax.optimization_barrier(v.astype(jnp.bfloat16)).astype(jnp.float32)

@jax.custom_vjp
def low_back(v):
    return v

def low_keep(v):
    return (low(v), None)

def low_pass(kept, grad):
    return (grad,)

def back_keep(v):
    return (v, None)

def back_low(kept, grad):
    return (low(grad),)
low.defvjp(low_keep, low_pass)
low_back.defvjp(back_keep, back_low)
EPSILON = 1e-05
HIGHEST_PRECISION = lax.Precision.HIGHEST

def layer_norm(rows_in, gain_vec, bias_vec):
    row_mean = lax.optimization_barrier(jnp.mean(rows_in, axis=-1, keepdims=True))
    centered = rows_in - row_mean
    spread = lax.optimization_barrier(jnp.mean(centered * centered, axis=-1, keepdims=True))
    return centered * lax.rsqrt(spread + EPSILON) * gain_vec + bias_vec

def one_sequence(seq_tokens, segment, params):
    ln1_gain, ln1_bias, qkv_weight, qkv_bias, out_weight, out_bias, ln2_gain, ln2_bias, fc_weight, fc_bias, proj_weight, proj_bias = params
    length = seq_tokens.shape[0]
    normed = low(layer_norm(seq_tokens, ln1_gain, ln1_bias))
    mixed_qkv = jnp.einsum('td,dce->tce', normed, qkv_weight, precision=HIGHEST_PRECISION) + qkv_bias
    mixed_qkv = low_back(low(mixed_qkv))
    queries = mixed_qkv[:, 0].reshape(length, H, HD)
    keys_all = mixed_qkv[:, 1].reshape(length, H, HD)
    values_all = mixed_qkv[:, 2].reshape(length, H, HD)
    scores = low_back(jnp.einsum('qhe,khe->hqk', queries, keys_all, precision=HIGHEST_PRECISION) * HD ** (-0.5))
    position = jnp.arange(length, dtype=jnp.int32)
    allowed = (position[None, :] <= position[:, None]) & (segment[None, :] == segment[:, None])
    scores = jnp.where(allowed[None], scores, -1e+30)
    attn_probs = low(jax.nn.softmax(scores, axis=-1))
    attended = jnp.einsum('hqk,khe->qhe', attn_probs, values_all, precision=HIGHEST_PRECISION).reshape(length, H * HD)
    attended = low_back(low(attended))
    middle = seq_tokens + low_back(jnp.dot(attended, out_weight, precision=HIGHEST_PRECISION)) + out_bias
    normed_two = low(layer_norm(middle, ln2_gain, ln2_bias))
    upward = low_back(jnp.dot(normed_two, fc_weight, precision=HIGHEST_PRECISION) + fc_bias)
    hidden = low(jax.nn.gelu(upward, approximate=True))
    return middle + low_back(jnp.dot(hidden, proj_weight, precision=HIGHEST_PRECISION)) + proj_bias

def reference(tokens, segments, ln1_gain, ln1_bias, qkv_weight, qkv_bias, out_weight, out_bias, ln2_gain, ln2_bias, fc_weight, fc_bias, proj_weight, proj_bias, grad_out):
    floats = tuple((argument_in.astype(jnp.float32) for argument_in in (ln1_gain, ln1_bias, qkv_weight, qkv_bias, out_weight, out_bias, ln2_gain, ln2_bias, fc_weight, fc_bias, proj_weight, proj_bias)))
    layer_step = jax.checkpoint(one_sequence)

    def forward(seq_block, *params):
        return lax.map(lambda element: layer_step(element[0], element[1], params), (seq_block, segments))
    block_out, pullback = jax.vjp(forward, tokens.astype(jnp.float32), *floats)
    gradients = pullback(grad_out.astype(jnp.float32))
    return (block_out.astype(jnp.bfloat16), gradients[0], gradients[1], gradients[2], gradients[3], gradients[4], gradients[5], gradients[6], gradients[7], gradients[8], gradients[9], gradients[10], gradients[11], gradients[12])
```

```python
import jax
import jax.numpy as jnp
from jax import lax
from jax.experimental import pallas as pl
from jax.experimental.pallas import tpu as pltpu
from jax.sharding import PartitionSpec as P

HD = 64


EPSILON = 1e-05
F32 = jnp.float32
BF16 = jnp.bfloat16
SCALE = HD ** (-0.5)


def normalize(rows_in, gain_vec, bias_vec):
    row_mean = jnp.mean(rows_in, axis=-1, keepdims=True)
    centered = rows_in - row_mean
    spread = jnp.mean(centered * centered, axis=-1, keepdims=True)
    inverse = lax.rsqrt(spread + EPSILON)
    scaled = centered * inverse
    return (scaled * gain_vec + bias_vec, scaled, inverse)


def normalize_back(grad_rows, scaled, inverse, gain_vec):
    weighted = grad_rows * gain_vec
    centered = weighted - jnp.mean(weighted, axis=-1, keepdims=True)
    return (centered - scaled * jnp.mean(weighted * scaled, axis=-1, keepdims=True)) * inverse


def gelu_tanh(values_in):
    return jax.nn.gelu(values_in, approximate=True)


def shifted(value, axis_name, step):
    count = lax.axis_size(axis_name)
    return lax.ppermute(value, axis_name, [(i, (i + step) % count) for i in range(count)])


def turned(value, axis_name, axis):
    count = lax.axis_size(axis_name)
    return jnp.concatenate(
        [value] + [shifted(value, axis_name, count - k) for k in range(1, count)], axis=axis
    )


def turned_sum(partial_value, axis_name, axis):
    count = lax.axis_size(axis_name)
    pieces = jnp.split(partial_value, count, axis=axis)
    total = pieces[0]
    for k in range(1, count):
        total = total + shifted(pieces[k].astype(BF16), axis_name, k).astype(F32)
    return total


def rounded(value):
    return lax.reduce_precision(value, 8, 7).astype(BF16)


def sum_everywhere(value, axis_name, axis):
    count = lax.axis_size(axis_name)
    index = lax.axis_index(axis_name)
    size = value.shape[axis] // count

    def block_of(k):
        return lax.dynamic_slice_in_dim(value, lax.rem(index + k, count) * size, size, axis)

    total = block_of(0)
    for k in range(1, count):
        total = total + shifted(block_of(k).astype(BF16), axis_name, k).astype(F32)
    total = rounded(total)
    result = jnp.zeros(value.shape, F32)
    for k in range(count):
        piece = total if k == 0 else shifted(total, axis_name, count - k)
        result = lax.dynamic_update_slice_in_dim(
            result, piece.astype(F32), lax.rem(index + k, count) * size, axis
        )
    return result


def sum_small(value, axis_names):
    for axis_name in axis_names:
        count = lax.axis_size(axis_name)
        step = 1
        while step < count:
            value = value + lax.ppermute(
                value, axis_name, [(i, i ^ step) for i in range(count)]
            )
            step *= 2
    return value


def dot(a, b, contract):
    return lax.dot_general(a, b, (contract, ((), ())), preferred_element_type=F32)


def attend_kernel(q_ref, kv_ref, qpos_ref, qseg_ref, kpos_ref, kseg_ref, att_ref, log_ref):
    width = q_ref.shape[2]
    allowed = (kpos_ref[0] <= qpos_ref[0]) & (kseg_ref[0] == qseg_ref[0])
    for h in range(width // HD):
        cols = slice(h * HD, (h + 1) * HD)
        vcols = slice(width + h * HD, width + (h + 1) * HD)
        scores = dot(kv_ref[0, :, cols], q_ref[0, :, cols], ((1,), (1,))) * SCALE
        scores = jnp.where(allowed, scores, -1e30)
        highest = jnp.max(scores, axis=0, keepdims=True)
        exponent = jnp.exp(scores - highest)
        denominator = jnp.sum(exponent, axis=0, keepdims=True)
        probs = (exponent * (1.0 / denominator)).astype(BF16)
        att_ref[0, :, cols] = dot(probs, kv_ref[0, :, vcols], ((0,), (0,))).astype(BF16)
        log_ref[0, h : h + 1, :] = highest + jnp.log(denominator)


def attend_back_kernel(
    q_ref, kv_ref, ga_ref, log_ref, qpos_ref, qseg_ref, kpos_ref, kseg_ref, gq_ref, gkv_ref
):
    width = q_ref.shape[2]
    allowed = (kpos_ref[0] <= qpos_ref[0]) & (kseg_ref[0] == qseg_ref[0])
    for h in range(width // HD):
        cols = slice(h * HD, (h + 1) * HD)
        vcols = slice(width + h * HD, width + (h + 1) * HD)
        query = q_ref[0, :, cols]
        keys = kv_ref[0, :, cols]
        grad = ga_ref[0, :, cols]
        scores = dot(keys, query, ((1,), (1,))) * SCALE
        probs = jnp.exp(jnp.where(allowed, scores, -1e30) - log_ref[0, h : h + 1, :])
        grad_probs = dot(kv_ref[0, :, vcols], grad, ((1,), (1,)))
        inner = jnp.sum(probs * grad_probs, axis=0, keepdims=True)
        grad_scores = (probs * (grad_probs - inner)).astype(BF16)
        gq_ref[0, :, cols] = (dot(grad_scores, keys, ((0,), (0,))) * SCALE).astype(BF16)
        gkv_ref[0, :, cols] = (dot(grad_scores, query, ((1,), (0,))) * SCALE).astype(BF16)
        gkv_ref[0, :, vcols] = dot(probs.astype(BF16), grad, ((1,), (0,))).astype(BF16)


def per_sequence(kernel, outs, *operands):
    def spec(shape):
        return pl.BlockSpec((1,) + tuple(shape[1:]), lambda s: (s,) + (0,) * (len(shape) - 1))

    return pl.pallas_call(
        kernel,
        grid=(operands[0].shape[0],),
        in_specs=[spec(o.shape) for o in operands],
        out_specs=[spec(o.shape) for o in outs],
        out_shape=outs,
        compiler_params=pltpu.CompilerParams(vmem_limit_bytes=48 * 1024 * 1024),
        cost_estimate=pl.CostEstimate(flops=2 * 10**9, bytes_accessed=8 * 10**6, transcendentals=0),
    )(*operands)


def shards(
    tokens,
    segments,
    ln1_gain,
    ln1_bias,
    qkv_weight,
    qkv_bias,
    out_weight,
    out_bias,
    ln2_gain,
    ln2_bias,
    fc_weight,
    fc_bias,
    proj_weight,
    proj_bias,
    grad_out,
):
    seq_count, shard_len, model_width = tokens.shape
    tp_count, ctx_count, dp_count = (lax.axis_size(n) for n in ("tp", "ctx", "dp"))
    tp_index, ctx_index, dp_index = (lax.axis_index(n) for n in ("tp", "ctx", "dp"))
    block_len = shard_len * tp_count
    key_len = block_len * ctx_count
    width_tp = qkv_weight.shape[2]
    piece = model_width // dp_count
    own_rows = seq_count * shard_len

    def turn(value, back=False):
        if dp_count == 1:
            return value
        start = dp_index * piece
        if back:
            start = lax.rem(model_width - start, model_width)
        return lax.dynamic_slice_in_dim(
            jnp.concatenate([value, value], axis=-1), start, model_width, value.ndim - 1
        )

    residual_in = turn(tokens.reshape(own_rows, model_width)).astype(F32)
    grad_low = turn(grad_out.reshape(own_rows, model_width))
    ln1_gain, ln1_bias, out_bias, ln2_gain, ln2_bias, proj_bias = [
        turn(v) for v in (ln1_gain, ln1_bias, out_bias, ln2_gain, ln2_bias, proj_bias)
    ]

    normed_one, scaled_one, inverse_one = normalize(residual_in, ln1_gain, ln1_bias)
    attn_rows = turned(normed_one.astype(BF16), "tp", 0)
    qkv_flat = jnp.concatenate([qkv_weight[:, c] for c in range(3)], axis=1)
    qkv_full = turned(qkv_flat, "dp", 0)
    out_full = turned(out_weight, "dp", 1)
    fc_full = turned(fc_weight, "dp", 0)
    proj_full = turned(proj_weight, "dp", 1)
    grad_rows = turned(grad_low, "tp", 0)

    def by_sequence(rows):
        width = rows.shape[1]
        rows = rows.reshape(tp_count, seq_count, shard_len, width)
        return rows.transpose(1, 0, 2, 3).reshape(seq_count, block_len, width)

    def by_rows(rows):
        width = rows.shape[2]
        rows = rows.reshape(seq_count, tp_count, shard_len, width)
        return rows.transpose(1, 0, 2, 3).reshape(tp_count * own_rows, width)

    mixed = (dot(attn_rows, qkv_full, ((1,), (0,))) + qkv_bias.reshape(-1)).astype(BF16)
    mixed = by_sequence(mixed)
    queries = mixed[:, :, :width_tp]
    own_pairs = mixed[:, :, width_tp:]
    key_value = jnp.concatenate(
        [own_pairs]
        + [
            lax.ppermute(own_pairs, "ctx", [(i, i + k) for i in range(ctx_count - k)])
            for k in range(1, ctx_count)
        ],
        axis=1,
    )

    within = jnp.arange(shard_len, dtype=jnp.int32)
    block_of = lax.rem(jnp.arange(tp_count, dtype=jnp.int32) + tp_index, tp_count)
    own_order = (block_of[:, None] * shard_len + within[None, :]).reshape(-1)
    query_pos = ctx_index * block_len + own_order
    key_block = ctx_index - jnp.arange(ctx_count, dtype=jnp.int32)
    key_start = jnp.where(key_block >= 0, key_block, ctx_count) * block_len
    key_pos = (key_start[:, None] + own_order[None, :]).reshape(-1)
    key_seg = segments.reshape(seq_count, ctx_count, tp_count, shard_len)
    key_seg = lax.dynamic_slice_in_dim(
        jnp.concatenate([key_seg, key_seg], axis=2), tp_index, tp_count, 2
    )
    key_seg = key_seg[:, ::-1]
    key_seg = lax.dynamic_slice_in_dim(
        jnp.concatenate([key_seg, key_seg], axis=1), ctx_count - 1 - ctx_index, ctx_count, 1
    ).reshape(seq_count, key_len)
    query_seg = key_seg[:, :block_len]
    places = (
        jnp.broadcast_to(query_pos[None, None, :], (seq_count, 1, block_len)),
        query_seg[:, None, :],
        jnp.broadcast_to(key_pos[None, :, None], (seq_count, key_len, 1)),
        key_seg[:, :, None],
    )
    heads = width_tp // HD
    attended, log_totals = per_sequence(
        attend_kernel,
        [
            jax.ShapeDtypeStruct((seq_count, block_len, width_tp), BF16),
            jax.ShapeDtypeStruct((seq_count, heads, block_len), F32),
        ],
        queries,
        key_value,
        *places,
    )
    attended_flat = by_rows(attended)
    branch = turned_sum(dot(attended_flat, out_full, ((1,), (0,))), "tp", 0)
    middle = residual_in + branch + out_bias
    normed_two, scaled_two, inverse_two = normalize(middle, ln2_gain, ln2_bias)
    mlp_rows = turned(normed_two.astype(BF16), "tp", 0)
    upward = dot(mlp_rows, fc_full, ((1,), (0,))) + fc_bias
    hidden, gelu_back = jax.vjp(gelu_tanh, upward)
    hidden_low = hidden.astype(BF16)

    grad_hidden = dot(grad_rows, proj_full, ((1,), (1,)))
    grad_up = gelu_back(grad_hidden)[0].astype(BF16)
    fc_bias_part = jnp.sum(grad_up, axis=0, dtype=F32)
    grad_normed_two = turned_sum(dot(grad_up, fc_full, ((1,), (1,))), "tp", 0)
    mlp_out = turned_sum(dot(hidden_low, proj_full, ((1,), (0,))), "tp", 0)
    block_out = turn((middle + mlp_out + proj_bias).astype(BF16), True)

    def over_dp(full, axis):
        return turned_sum(full, "dp", axis)

    proj_grad = over_dp(dot(hidden_low, grad_rows, ((0,), (0,))), 1)
    fc_grad = over_dp(dot(mlp_rows, grad_up, ((0,), (0,))), 0)
    proj_weight_grad = sum_everywhere(proj_grad, "ctx", 0)
    fc_weight_grad = sum_everywhere(fc_grad, "ctx", 0)

    grad_top = grad_low.astype(F32)
    grad_middle = grad_top + normalize_back(grad_normed_two, scaled_two, inverse_two, ln2_gain)
    middle_rows = turned(grad_middle.astype(BF16), "tp", 0)
    grad_attended = by_sequence(dot(middle_rows, out_full, ((1,), (1,))).astype(BF16))
    out_grad = over_dp(dot(attended_flat, middle_rows, ((0,), (0,))), 1)
    out_weight_grad = sum_everywhere(out_grad, "ctx", 0)

    grad_queries, grad_pairs = per_sequence(
        attend_back_kernel,
        [
            jax.ShapeDtypeStruct((seq_count, block_len, width_tp), BF16),
            jax.ShapeDtypeStruct((seq_count, key_len, 2 * width_tp), BF16),
        ],
        queries,
        key_value,
        grad_attended,
        log_totals,
        *places,
    )

    def pair_block(k):
        return grad_pairs[:, k * block_len : (k + 1) * block_len]

    grad_pairs_own = pair_block(0).astype(F32)
    for k in range(1, ctx_count):
        grad_pairs_own = grad_pairs_own + lax.ppermute(
            pair_block(k), "ctx", [(i, i - k) for i in range(k, ctx_count)]
        ).astype(F32)
    grad_mixed = by_rows(
        jnp.concatenate([grad_queries, grad_pairs_own.astype(BF16)], axis=2)
    )
    qkv_bias_part = jnp.sum(grad_mixed, axis=0, dtype=F32)
    qkv_grad = over_dp(dot(attn_rows, grad_mixed, ((0,), (0,))), 0)
    qkv_grad = sum_everywhere(qkv_grad, "ctx", 0)
    qkv_weight_grad = jnp.stack(jnp.split(qkv_grad, 3, axis=1), axis=1)
    grad_normed_one = turned_sum(dot(grad_mixed, qkv_full, ((1,), (1,))), "tp", 0)
    tokens_grad = grad_middle + normalize_back(grad_normed_one, scaled_one, inverse_one, ln1_gain)

    shared = jnp.stack(
        [
            jnp.sum(grad_normed_one * scaled_one, axis=0),
            jnp.sum(grad_normed_one, axis=0),
            jnp.sum(grad_middle, axis=0),
            jnp.sum(grad_normed_two * scaled_two, axis=0),
            jnp.sum(grad_normed_two, axis=0),
            jnp.sum(grad_top, axis=0),
        ]
    )
    shared = sum_small(turn(shared, True), ("dp", "ctx", "tp"))
    split_biases = sum_small(jnp.concatenate([qkv_bias_part, fc_bias_part]), ("dp", "ctx"))
    qkv_bias_grad = split_biases[: 3 * width_tp].reshape(3, width_tp)
    fc_bias_grad = split_biases[3 * width_tp :]
    ln1_gain_grad, ln1_bias_grad, out_bias_grad, ln2_gain_grad, ln2_bias_grad, proj_bias_grad = [
        shared[i] for i in range(6)
    ]
    return (
        block_out.reshape(tokens.shape),
        turn(tokens_grad, True).reshape(tokens.shape),
        ln1_gain_grad,
        ln1_bias_grad,
        qkv_weight_grad,
        qkv_bias_grad,
        out_weight_grad,
        out_bias_grad,
        ln2_gain_grad,
        ln2_bias_grad,
        fc_weight_grad,
        fc_bias_grad,
        proj_weight_grad,
        proj_bias_grad,
    )


def solution(mesh):
    placed = (
        P("dp", ("ctx", "tp"), None),
        P("dp", None),
        P(),
        P(),
        P("dp", None, "tp"),
        P(None, "tp"),
        P("tp", "dp"),
        P(),
        P(),
        P(),
        P("dp", "tp"),
        P("tp"),
        P("tp", "dp"),
        P(),
        P("dp", ("ctx", "tp"), None),
    )
    return jax.shard_map(
        shards,
        mesh=mesh,
        in_specs=placed,
        out_specs=(
            P("dp", ("ctx", "tp"), None),
            P("dp", ("ctx", "tp"), None),
            P(),
            P(),
            P("dp", None, "tp"),
            P(None, "tp"),
            P("tp", "dp"),
            P(),
            P(),
            P(),
            P("dp", "tp"),
            P("tp"),
            P("tp", "dp"),
            P(),
        ),
        check_vma=False,
    )
```

```python
import functools

import jax
import jax.numpy as jnp
from jax import lax
from jax.experimental import pallas as pl
from jax.experimental.pallas import tpu as pltpu
from jax.sharding import PartitionSpec as P

HD = 64


EPSILON = 1e-05
F32 = jnp.float32
BF16 = jnp.bfloat16
SCALE = HD ** (-0.5)


def normalize(rows_in, gain_vec, bias_vec):
    row_mean = jnp.mean(rows_in, axis=-1, keepdims=True)
    centered = rows_in - row_mean
    spread = jnp.mean(centered * centered, axis=-1, keepdims=True)
    inverse = lax.rsqrt(spread + EPSILON)
    scaled = centered * inverse
    return (scaled * gain_vec + bias_vec, scaled, inverse)


def normalize_back(grad_rows, scaled, inverse, gain_vec):
    weighted = grad_rows * gain_vec
    centered = weighted - jnp.mean(weighted, axis=-1, keepdims=True)
    return (centered - scaled * jnp.mean(weighted * scaled, axis=-1, keepdims=True)) * inverse


def gelu_tanh(values_in):
    return jax.nn.gelu(values_in, approximate=True)


def shifted(value, axis_name, step):
    count = lax.axis_size(axis_name)
    return lax.ppermute(value, axis_name, [(i, (i + step) % count) for i in range(count)])


def turned(value, axis_name, axis):
    count = lax.axis_size(axis_name)
    return jnp.concatenate(
        [value] + [shifted(value, axis_name, count - k) for k in range(1, count)], axis=axis
    )


def turned_sum(partial_value, axis_name, axis):
    count = lax.axis_size(axis_name)
    pieces = jnp.split(partial_value, count, axis=axis)
    total = pieces[0]
    for k in range(1, count):
        total = total + shifted(pieces[k].astype(BF16), axis_name, k).astype(F32)
    return total


def rounded(value):
    return lax.reduce_precision(value, 8, 7).astype(BF16)


def sum_everywhere(value, axis_name, axis):
    count = lax.axis_size(axis_name)
    index = lax.axis_index(axis_name)
    steps = [1 << i for i in range(count.bit_length() - 1)]

    def swap(piece, step):
        return lax.ppermute(piece, axis_name, [(i, i ^ step) for i in range(count)])

    for step in steps:
        bit = lax.rem(index // step, 2)
        size = value.shape[axis] // 2
        other = lax.dynamic_slice_in_dim(value, (1 - bit) * size, size, axis).astype(BF16)
        own = lax.dynamic_slice_in_dim(value, bit * size, size, axis)
        value = own + swap(other, step).astype(F32)
    value = rounded(value)
    for step in reversed(steps):
        bit = lax.rem(index // step, 2)
        size = value.shape[axis]
        other = swap(value, step)
        low = jnp.where(bit == 0, value, other)
        high = jnp.where(bit == 0, other, value)
        value = jnp.concatenate([low, high], axis=axis)
    return value.astype(F32)


def greet(axis_name, count, index):
    barrier = pltpu.get_barrier_semaphore()
    for k in range(1, count):
        pl.semaphore_signal(
            barrier,
            inc=1,
            device_id={axis_name: lax.rem(index + k, count)},
            device_id_type=pl.DeviceIdType.MESH,
        )
    pl.semaphore_wait(barrier, count - 1)


def gather_kernel(axis_name, count, x_ref, o_ref, send_sem, recv_sem, own_sem):
    index = lax.axis_index(axis_name)
    own = pltpu.make_async_copy(x_ref, o_ref.at[0], own_sem)
    own.start()
    greet(axis_name, count, index)
    copies = []
    for k in range(1, count):
        copies.append(
            pltpu.make_async_remote_copy(
                src_ref=x_ref,
                dst_ref=o_ref.at[k],
                send_sem=send_sem.at[k],
                recv_sem=recv_sem.at[k],
                device_id={axis_name: lax.rem(index + count - k, count)},
                device_id_type=pl.DeviceIdType.MESH,
            )
        )
        copies[-1].start()
    for copy in copies:
        copy.wait()
    own.wait()


def scatter_kernel(axis_name, count, x_ref, o_ref, send_sem, recv_sem, own_sem):
    index = lax.axis_index(axis_name)
    own = pltpu.make_async_copy(x_ref.at[0], o_ref.at[0], own_sem)
    own.start()
    greet(axis_name, count, index)
    copies = []
    for k in range(1, count):
        copies.append(
            pltpu.make_async_remote_copy(
                src_ref=x_ref.at[k],
                dst_ref=o_ref.at[k],
                send_sem=send_sem.at[k],
                recv_sem=recv_sem.at[k],
                device_id={axis_name: lax.rem(index + k, count)},
                device_id_type=pl.DeviceIdType.MESH,
            )
        )
        copies[-1].start()
    for copy in copies:
        copy.wait()
    own.wait()


def swap_kernel(axis_name, count, x_ref, o_ref, send_sem, recv_sem, own_sem):
    index = lax.axis_index(axis_name)
    own = pltpu.make_async_copy(x_ref.at[index], o_ref.at[index], own_sem)
    own.start()
    greet(axis_name, count, index)
    copies = []
    for k in range(1, count):
        target = lax.rem(index + k, count)
        copies.append(
            pltpu.make_async_remote_copy(
                src_ref=x_ref.at[target],
                dst_ref=o_ref.at[index],
                send_sem=send_sem.at[k],
                recv_sem=recv_sem.at[k],
                device_id={axis_name: target},
                device_id_type=pl.DeviceIdType.MESH,
            )
        )
        copies[-1].start()
    for copy in copies:
        copy.wait()
    own.wait()


def exchange(kernel, value, axis_name, collective_id):
    count = lax.axis_size(axis_name)
    shape = value.shape if value.ndim == 3 else (count,) + value.shape
    return pl.pallas_call(
        functools.partial(kernel, axis_name, count),
        out_shape=jax.ShapeDtypeStruct(shape, value.dtype),
        in_specs=[pl.BlockSpec(memory_space=pl.ANY)],
        out_specs=pl.BlockSpec(memory_space=pl.ANY),
        scratch_shapes=[
            pltpu.SemaphoreType.DMA((count,)),
            pltpu.SemaphoreType.DMA((count,)),
            pltpu.SemaphoreType.DMA,
        ],
        compiler_params=pltpu.CompilerParams(collective_id=collective_id, has_side_effects=True),
        cost_estimate=pl.CostEstimate(flops=0, bytes_accessed=10 * 10**6, transcendentals=0),
    )(value)


def gathered(rows):
    return exchange(gather_kernel, rows, "tp", 0).reshape(-1, rows.shape[1])


def scattered_sum(partial_value):
    count = lax.axis_size("tp")
    pieces = partial_value.reshape(count, -1, partial_value.shape[1]).astype(BF16)
    return jnp.sum(exchange(scatter_kernel, pieces, "tp", 1).astype(F32), axis=0)


def sum_small(value, axis_names):
    for axis_name in axis_names:
        count = lax.axis_size(axis_name)
        step = 1
        while step < count:
            value = value + lax.ppermute(
                value, axis_name, [(i, i ^ step) for i in range(count)]
            )
            step *= 2
    return value


def dot(a, b, contract):
    return lax.dot_general(a, b, (contract, ((), ())), preferred_element_type=F32)


def attend_kernel(qkv_ref, qpos_ref, qseg_ref, kpos_ref, kseg_ref, att_ref, log_ref):
    blocks, block_len, width = qkv_ref.shape
    width //= 3
    heads = width // HD
    for i in range(blocks):
        keep = (i + 1) * block_len
        allowed = (kpos_ref[:keep] <= qpos_ref[i : i + 1]) & (kseg_ref[:keep] == qseg_ref[i : i + 1])
        for h in range(heads):
            cols = slice(h * HD, (h + 1) * HD)
            kcols = slice(width + h * HD, width + (h + 1) * HD)
            vcols = slice(2 * width + h * HD, 2 * width + (h + 1) * HD)
            keys = qkv_ref[: i + 1, :, kcols].reshape(keep, HD)
            values = qkv_ref[: i + 1, :, vcols].reshape(keep, HD)
            scores = dot(keys, qkv_ref[i, :, cols], ((1,), (1,))) * SCALE
            scores = jnp.where(allowed, scores, -1e30)
            highest = jnp.max(scores, axis=0, keepdims=True)
            exponent = jnp.exp(scores - highest)
            denominator = jnp.sum(exponent, axis=0, keepdims=True)
            probs = (exponent * (1.0 / denominator)).astype(BF16)
            att_ref[i, :, cols] = dot(probs, values, ((0,), (0,))).astype(BF16)
            row = i * heads + h
            log_ref[row : row + 1, :] = highest + jnp.log(denominator)


def attend_back_kernel(
    qkv_ref, ga_ref, log_ref, qpos_ref, qseg_ref, kpos_ref, kseg_ref, grad_ref, gk_ref, gv_ref
):
    blocks, block_len, width = qkv_ref.shape
    width //= 3
    heads = width // HD
    for i in reversed(range(blocks)):
        keep = (i + 1) * block_len
        allowed = (kpos_ref[:keep] <= qpos_ref[i : i + 1]) & (kseg_ref[:keep] == qseg_ref[i : i + 1])
        for h in range(heads):
            cols = slice(h * HD, (h + 1) * HD)
            kcols = slice(width + h * HD, width + (h + 1) * HD)
            vcols = slice(2 * width + h * HD, 2 * width + (h + 1) * HD)
            query = qkv_ref[i, :, cols]
            keys = qkv_ref[: i + 1, :, kcols].reshape(keep, HD)
            values = qkv_ref[: i + 1, :, vcols].reshape(keep, HD)
            grad = ga_ref[i, :, cols]
            row = i * heads + h
            scores = dot(keys, query, ((1,), (1,))) * SCALE
            probs = jnp.exp(jnp.where(allowed, scores, -1e30) - log_ref[row : row + 1, :])
            grad_probs = dot(values, grad, ((1,), (1,)))
            inner = jnp.sum(probs * grad_probs, axis=0, keepdims=True)
            grad_scores = (probs * (grad_probs - inner)).astype(BF16)
            grad_ref[i, :, cols] = (dot(grad_scores, keys, ((0,), (0,))) * SCALE).astype(BF16)
            grad_keys = dot(grad_scores, query, ((1,), (0,))) * SCALE
            grad_values = dot(probs.astype(BF16), grad, ((1,), (0,)))
            if i == blocks - 1:
                gk_ref[:keep, cols] = grad_keys
                gv_ref[:keep, cols] = grad_values
            else:
                gk_ref[:keep, cols] += grad_keys
                gv_ref[:keep, cols] += grad_values
    shape = (blocks, block_len, width)
    grad_ref[:, :, width : 2 * width] = gk_ref[...].reshape(shape).astype(BF16)
    grad_ref[:, :, 2 * width :] = gv_ref[...].reshape(shape).astype(BF16)


def local_call(kernel, outs, scratch, *operands):
    whole = pl.BlockSpec(memory_space=pltpu.VMEM)
    return pl.pallas_call(
        kernel,
        in_specs=[whole] * len(operands),
        out_specs=[whole] * len(outs),
        out_shape=outs,
        scratch_shapes=scratch,
        compiler_params=pltpu.CompilerParams(vmem_limit_bytes=48 * 1024 * 1024),
        cost_estimate=pl.CostEstimate(flops=4 * 10**9, bytes_accessed=8 * 10**6, transcendentals=0),
    )(*operands)


def shards(
    tokens,
    segments,
    ln1_gain,
    ln1_bias,
    qkv_weight,
    qkv_bias,
    out_weight,
    out_bias,
    ln2_gain,
    ln2_bias,
    fc_weight,
    fc_bias,
    proj_weight,
    proj_bias,
    grad_out,
):
    seq_count, shard_len, model_width = tokens.shape
    tp_count, ctx_count, dp_count = (lax.axis_size(n) for n in ("tp", "ctx", "dp"))
    tp_index, ctx_index, dp_index = (lax.axis_index(n) for n in ("tp", "ctx", "dp"))
    block_len = shard_len * tp_count
    key_len = block_len * ctx_count
    width_tp = qkv_weight.shape[2]
    piece = model_width // dp_count
    own_rows = seq_count * shard_len

    def turn(value, back=False):
        if dp_count == 1:
            return value
        start = dp_index * piece
        if back:
            start = lax.rem(model_width - start, model_width)
        return lax.dynamic_slice_in_dim(
            jnp.concatenate([value, value], axis=-1), start, model_width, value.ndim - 1
        )

    residual_in = turn(tokens.reshape(own_rows, model_width)).astype(F32)
    grad_low = turn(grad_out.reshape(own_rows, model_width))
    ln1_gain, ln1_bias, out_bias, ln2_gain, ln2_bias, proj_bias = [
        turn(v) for v in (ln1_gain, ln1_bias, out_bias, ln2_gain, ln2_bias, proj_bias)
    ]

    normed_one, scaled_one, inverse_one = normalize(residual_in, ln1_gain, ln1_bias)
    attn_rows = gathered(normed_one.astype(BF16))
    qkv_flat = jnp.concatenate([qkv_weight[:, c] for c in range(3)], axis=1)
    qkv_full = turned(qkv_flat, "dp", 0)
    out_full = turned(out_weight, "dp", 1)
    fc_full = turned(fc_weight, "dp", 0)
    proj_full = turned(proj_weight, "dp", 1)
    grad_rows = turned(grad_low, "tp", 0)

    per_seq = ctx_count // seq_count
    group_width = width_tp // per_seq

    def by_group(rows, parts):
        rows = rows.reshape(tp_count, seq_count, shard_len, parts, per_seq, group_width)
        rows = rows.transpose(1, 4, 0, 2, 3, 5)
        return rows.reshape(ctx_count, block_len, parts * group_width)

    def by_rows(groups, parts):
        groups = groups.reshape(seq_count, per_seq, tp_count, shard_len, parts, group_width)
        groups = groups.transpose(2, 0, 3, 4, 1, 5)
        return groups.reshape(tp_count * own_rows, parts * width_tp)

    mixed = (dot(attn_rows, qkv_full, ((1,), (0,))) + qkv_bias.reshape(-1)).astype(BF16)
    mixed = exchange(swap_kernel, by_group(mixed, 3), "ctx", 2)

    within = jnp.arange(shard_len, dtype=jnp.int32)
    block_of = lax.rem(jnp.arange(tp_count, dtype=jnp.int32) + tp_index, tp_count)
    own_order = (block_of[:, None] * shard_len + within[None, :]).reshape(-1)
    places = jnp.arange(ctx_count, dtype=jnp.int32)[:, None] * block_len + own_order[None, :]
    document = lax.dynamic_index_in_dim(segments, ctx_index // per_seq, 0, False)
    document = document.reshape(ctx_count, tp_count, shard_len)
    document = lax.dynamic_slice_in_dim(
        jnp.concatenate([document, document], axis=1), tp_index, tp_count, 1
    ).reshape(ctx_count, block_len)
    places = (places, document, places.reshape(key_len, 1), document.reshape(key_len, 1))
    attended, log_totals = local_call(
        attend_kernel,
        [
            jax.ShapeDtypeStruct((ctx_count, block_len, group_width), BF16),
            jax.ShapeDtypeStruct((ctx_count * (group_width // HD), block_len), F32),
        ],
        [],
        mixed,
        *places,
    )
    attended_flat = by_rows(exchange(swap_kernel, attended, "ctx", 3), 1)
    branch = scattered_sum(dot(attended_flat, out_full, ((1,), (0,))))
    middle = residual_in + branch + out_bias
    normed_two, scaled_two, inverse_two = normalize(middle, ln2_gain, ln2_bias)
    mlp_rows = gathered(normed_two.astype(BF16))
    upward = dot(mlp_rows, fc_full, ((1,), (0,))) + fc_bias
    hidden, gelu_back = jax.vjp(gelu_tanh, upward)
    hidden_low = hidden.astype(BF16)

    grad_hidden = dot(grad_rows, proj_full, ((1,), (1,)))
    grad_up = gelu_back(grad_hidden)[0].astype(BF16)
    fc_bias_part = jnp.sum(grad_up, axis=0, dtype=F32)
    grad_normed_two = scattered_sum(dot(grad_up, fc_full, ((1,), (1,))))
    mlp_out = turned_sum(dot(hidden_low, proj_full, ((1,), (0,))), "tp", 0)
    block_out = turn((middle + mlp_out + proj_bias).astype(BF16), True)

    def over_dp(full, axis):
        return turned_sum(full, "dp", axis)

    proj_grad = over_dp(dot(hidden_low, grad_rows, ((0,), (0,))), 1)
    fc_grad = over_dp(dot(mlp_rows, grad_up, ((0,), (0,))), 0)
    proj_weight_grad = sum_everywhere(proj_grad, "ctx", 0)
    fc_weight_grad = sum_everywhere(fc_grad, "ctx", 0)

    grad_top = grad_low.astype(F32)
    grad_middle = grad_top + normalize_back(grad_normed_two, scaled_two, inverse_two, ln2_gain)
    middle_rows = gathered(grad_middle.astype(BF16))
    grad_attended = by_group(dot(middle_rows, out_full, ((1,), (1,))).astype(BF16), 1)
    grad_attended = exchange(swap_kernel, grad_attended, "ctx", 3)
    out_grad = over_dp(dot(attended_flat, middle_rows, ((0,), (0,))), 1)
    out_weight_grad = sum_everywhere(out_grad, "ctx", 0)

    (grad_groups,) = local_call(
        attend_back_kernel,
        [jax.ShapeDtypeStruct(mixed.shape, BF16)],
        [pltpu.VMEM((key_len, group_width), F32)] * 2,
        mixed,
        grad_attended,
        log_totals,
        *places,
    )
    grad_mixed = by_rows(exchange(swap_kernel, grad_groups, "ctx", 2), 3)
    qkv_bias_part = jnp.sum(grad_mixed, axis=0, dtype=F32)
    qkv_grad = over_dp(dot(attn_rows, grad_mixed, ((0,), (0,))), 0)
    qkv_grad = sum_everywhere(qkv_grad, "ctx", 0)
    qkv_weight_grad = jnp.stack(jnp.split(qkv_grad, 3, axis=1), axis=1)
    grad_normed_one = scattered_sum(dot(grad_mixed, qkv_full, ((1,), (1,))))
    tokens_grad = grad_middle + normalize_back(grad_normed_one, scaled_one, inverse_one, ln1_gain)

    shared = jnp.stack(
        [
            jnp.sum(grad_normed_one * scaled_one, axis=0),
            jnp.sum(grad_normed_one, axis=0),
            jnp.sum(grad_middle, axis=0),
            jnp.sum(grad_normed_two * scaled_two, axis=0),
            jnp.sum(grad_normed_two, axis=0),
            jnp.sum(grad_top, axis=0),
        ]
    )
    shared = sum_small(turn(shared, True), ("dp", "ctx", "tp"))
    split_biases = sum_small(jnp.concatenate([qkv_bias_part, fc_bias_part]), ("dp", "ctx"))
    qkv_bias_grad = split_biases[: 3 * width_tp].reshape(3, width_tp)
    fc_bias_grad = split_biases[3 * width_tp :]
    ln1_gain_grad, ln1_bias_grad, out_bias_grad, ln2_gain_grad, ln2_bias_grad, proj_bias_grad = [
        shared[i] for i in range(6)
    ]
    return (
        block_out.reshape(tokens.shape),
        turn(tokens_grad, True).reshape(tokens.shape),
        ln1_gain_grad,
        ln1_bias_grad,
        qkv_weight_grad,
        qkv_bias_grad,
        out_weight_grad,
        out_bias_grad,
        ln2_gain_grad,
        ln2_bias_grad,
        fc_weight_grad,
        fc_bias_grad,
        proj_weight_grad,
        proj_bias_grad,
    )


def solution(mesh):
    placed = (
        P("dp", ("ctx", "tp"), None),
        P("dp", None),
        P(),
        P(),
        P("dp", None, "tp"),
        P(None, "tp"),
        P("tp", "dp"),
        P(),
        P(),
        P(),
        P("dp", "tp"),
        P("tp"),
        P("tp", "dp"),
        P(),
        P("dp", ("ctx", "tp"), None),
    )
    return jax.shard_map(
        shards,
        mesh=mesh,
        in_specs=placed,
        out_specs=(
            P("dp", ("ctx", "tp"), None),
            P("dp", ("ctx", "tp"), None),
            P(),
            P(),
            P("dp", None, "tp"),
            P(None, "tp"),
            P("tp", "dp"),
            P(),
            P(),
            P(),
            P("dp", "tp"),
            P("tp"),
            P("tp", "dp"),
            P(),
        ),
        check_vma=False,
    )
```

```python
import functools

import jax
import jax.numpy as jnp
from jax import lax
from jax.experimental import pallas as pl
from jax.experimental.pallas import tpu as pltpu
from jax.sharding import PartitionSpec as P

HD = 64


EPSILON = 1e-05
F32 = jnp.float32
BF16 = jnp.bfloat16
SCALE = HD ** (-0.5)


def normalize(rows_in, gain_vec, bias_vec):
    row_mean = jnp.mean(rows_in, axis=-1, keepdims=True)
    centered = rows_in - row_mean
    spread = jnp.mean(centered * centered, axis=-1, keepdims=True)
    inverse = lax.rsqrt(spread + EPSILON)
    scaled = centered * inverse
    return (scaled * gain_vec + bias_vec, scaled, inverse)


def normalize_back(grad_rows, scaled, inverse, gain_vec):
    weighted = grad_rows * gain_vec
    centered = weighted - jnp.mean(weighted, axis=-1, keepdims=True)
    return (centered - scaled * jnp.mean(weighted * scaled, axis=-1, keepdims=True)) * inverse


def gelu_tanh(values_in):
    return jax.nn.gelu(values_in, approximate=True)


def shifted(value, axis_name, step):
    count = lax.axis_size(axis_name)
    return lax.ppermute(value, axis_name, [(i, (i + step) % count) for i in range(count)])


def turned(value, axis_name, axis):
    count = lax.axis_size(axis_name)
    return jnp.concatenate(
        [value] + [shifted(value, axis_name, count - k) for k in range(1, count)], axis=axis
    )


def turned_sum(partial_value, axis_name, axis):
    count = lax.axis_size(axis_name)
    pieces = jnp.split(partial_value, count, axis=axis)
    total = pieces[0]
    for k in range(1, count):
        total = total + shifted(pieces[k].astype(BF16), axis_name, k).astype(F32)
    return total


def rounded(value):
    return lax.reduce_precision(value, 8, 7).astype(BF16)


def weight_sum(full, dp_axis, ctx_axis):
    dp_count = lax.axis_size("dp")
    pieces = jnp.split(full, dp_count, axis=dp_axis)
    sent = [piece.astype(BF16) for piece in pieces[1:]]
    stages = [[shifted(piece, "dp", k + 1) for k, piece in enumerate(sent)]]
    value = pieces[0]
    for piece in stages[0]:
        value = value + piece.astype(F32)
    count = lax.axis_size("ctx")
    index = lax.axis_index("ctx")
    steps = [1 << i for i in range(count.bit_length() - 1)]

    def swap(piece, step):
        stages.append([lax.ppermute(piece, "ctx", [(i, i ^ step) for i in range(count)])])
        return stages[-1][0]

    for step in steps:
        bit = lax.rem(index // step, 2)
        size = value.shape[ctx_axis] // 2
        other = lax.dynamic_slice_in_dim(value, (1 - bit) * size, size, ctx_axis).astype(BF16)
        own = lax.dynamic_slice_in_dim(value, bit * size, size, ctx_axis)
        value = own + swap(other, step).astype(F32)
    value = rounded(value)
    for step in reversed(steps):
        bit = lax.rem(index // step, 2)
        other = swap(value, step)
        low = jnp.where(bit == 0, value, other)
        high = jnp.where(bit == 0, other, value)
        value = jnp.concatenate([low, high], axis=ctx_axis)
    return value.astype(F32), sent, stages


def greet(axis_name, count, index):
    barrier = pltpu.get_barrier_semaphore()
    for k in range(1, count):
        pl.semaphore_signal(
            barrier,
            inc=1,
            device_id={axis_name: lax.rem(index + k, count)},
            device_id_type=pl.DeviceIdType.MESH,
        )
    pl.semaphore_wait(barrier, count - 1)


def gather_kernel(axis_name, count, x_ref, *refs):
    o_ref, send_sem, recv_sem, own_sem = refs[-4:]
    index = lax.axis_index(axis_name)
    own = pltpu.make_async_copy(x_ref, o_ref.at[0], own_sem)
    own.start()
    greet(axis_name, count, index)
    copies = []
    for k in range(1, count):
        copies.append(
            pltpu.make_async_remote_copy(
                src_ref=x_ref,
                dst_ref=o_ref.at[k],
                send_sem=send_sem.at[k],
                recv_sem=recv_sem.at[k],
                device_id={axis_name: lax.rem(index + count - k, count)},
                device_id_type=pl.DeviceIdType.MESH,
            )
        )
        copies[-1].start()
    for copy in copies:
        copy.wait()
    own.wait()


def scatter_kernel(axis_name, count, x_ref, *refs):
    o_ref, send_sem, recv_sem, own_sem = refs[-4:]
    index = lax.axis_index(axis_name)
    own = pltpu.make_async_copy(x_ref.at[0], o_ref.at[0], own_sem)
    own.start()
    greet(axis_name, count, index)
    copies = []
    for k in range(1, count):
        copies.append(
            pltpu.make_async_remote_copy(
                src_ref=x_ref.at[k],
                dst_ref=o_ref.at[k],
                send_sem=send_sem.at[k],
                recv_sem=recv_sem.at[k],
                device_id={axis_name: lax.rem(index + k, count)},
                device_id_type=pl.DeviceIdType.MESH,
            )
        )
        copies[-1].start()
    for copy in copies:
        copy.wait()
    own.wait()


def swap_kernel(axis_name, count, x_ref, *refs):
    o_ref, send_sem, recv_sem, own_sem = refs[-4:]
    index = lax.axis_index(axis_name)
    own = pltpu.make_async_copy(x_ref.at[index], o_ref.at[index], own_sem)
    own.start()
    greet(axis_name, count, index)
    copies = []
    for k in range(1, count):
        target = lax.rem(index + k, count)
        copies.append(
            pltpu.make_async_remote_copy(
                src_ref=x_ref.at[target],
                dst_ref=o_ref.at[index],
                send_sem=send_sem.at[k],
                recv_sem=recv_sem.at[k],
                device_id={axis_name: target},
                device_id_type=pl.DeviceIdType.MESH,
            )
        )
        copies[-1].start()
    for copy in copies:
        copy.wait()
    own.wait()


def exchange(kernel, value, axis_name, collective_id, after=()):
    count = lax.axis_size(axis_name)
    shape = value.shape if value.ndim == 3 else (count,) + value.shape
    return pl.pallas_call(
        functools.partial(kernel, axis_name, count),
        out_shape=jax.ShapeDtypeStruct(shape, value.dtype),
        in_specs=[pl.BlockSpec(memory_space=pl.ANY)] * (1 + len(after)),
        out_specs=pl.BlockSpec(memory_space=pl.ANY),
        scratch_shapes=[
            pltpu.SemaphoreType.DMA((count,)),
            pltpu.SemaphoreType.DMA((count,)),
            pltpu.SemaphoreType.DMA,
        ],
        compiler_params=pltpu.CompilerParams(collective_id=collective_id, has_side_effects=True),
        cost_estimate=pl.CostEstimate(flops=0, bytes_accessed=50 * 10**6, transcendentals=0),
    )(value, *after)


def gathered(rows, collective_id, after=()):
    return exchange(gather_kernel, rows, "tp", collective_id, after).reshape(-1, rows.shape[1])


def scattered_sum(partial_value, collective_id, after=()):
    count = lax.axis_size("tp")
    pieces = partial_value.reshape(count, -1, partial_value.shape[1]).astype(BF16)
    received = exchange(scatter_kernel, pieces, "tp", collective_id, after)
    return jnp.sum(received.astype(F32), axis=0)


def sum_small(value, axis_names):
    for axis_name in axis_names:
        count = lax.axis_size(axis_name)
        step = 1
        while step < count:
            value = value + lax.ppermute(
                value, axis_name, [(i, i ^ step) for i in range(count)]
            )
            step *= 2
    return value


def dot(a, b, contract):
    return lax.dot_general(a, b, (contract, ((), ())), preferred_element_type=F32)


def attend_kernel(qkv_ref, qpos_ref, qseg_ref, kpos_ref, kseg_ref, att_ref, log_ref):
    blocks, block_len, width = qkv_ref.shape
    width //= 3
    heads = width // HD
    for i in range(blocks):
        keep = (i + 1) * block_len
        allowed = (kpos_ref[:keep] <= qpos_ref[i : i + 1]) & (kseg_ref[:keep] == qseg_ref[i : i + 1])
        for h in range(heads):
            cols = slice(h * HD, (h + 1) * HD)
            kcols = slice(width + h * HD, width + (h + 1) * HD)
            vcols = slice(2 * width + h * HD, 2 * width + (h + 1) * HD)
            keys = qkv_ref[: i + 1, :, kcols].reshape(keep, HD)
            values = qkv_ref[: i + 1, :, vcols].reshape(keep, HD)
            scores = dot(keys, qkv_ref[i, :, cols], ((1,), (1,))) * SCALE
            scores = jnp.where(allowed, scores, -1e30)
            highest = jnp.max(scores, axis=0, keepdims=True)
            exponent = jnp.exp(scores - highest)
            denominator = jnp.sum(exponent, axis=0, keepdims=True)
            probs = (exponent * (1.0 / denominator)).astype(BF16)
            att_ref[i, :, cols] = dot(probs, values, ((0,), (0,))).astype(BF16)
            row = i * heads + h
            log_ref[row : row + 1, :] = highest + jnp.log(denominator)


def attend_back_kernel(
    qkv_ref, ga_ref, log_ref, qpos_ref, qseg_ref, kpos_ref, kseg_ref, grad_ref, gk_ref, gv_ref
):
    blocks, block_len, width = qkv_ref.shape
    width //= 3
    heads = width // HD
    for i in reversed(range(blocks)):
        keep = (i + 1) * block_len
        allowed = (kpos_ref[:keep] <= qpos_ref[i : i + 1]) & (kseg_ref[:keep] == qseg_ref[i : i + 1])
        for h in range(heads):
            cols = slice(h * HD, (h + 1) * HD)
            kcols = slice(width + h * HD, width + (h + 1) * HD)
            vcols = slice(2 * width + h * HD, 2 * width + (h + 1) * HD)
            query = qkv_ref[i, :, cols]
            keys = qkv_ref[: i + 1, :, kcols].reshape(keep, HD)
            values = qkv_ref[: i + 1, :, vcols].reshape(keep, HD)
            grad = ga_ref[i, :, cols]
            row = i * heads + h
            scores = dot(keys, query, ((1,), (1,))) * SCALE
            probs = jnp.exp(jnp.where(allowed, scores, -1e30) - log_ref[row : row + 1, :])
            grad_probs = dot(values, grad, ((1,), (1,)))
            inner = jnp.sum(probs * grad_probs, axis=0, keepdims=True)
            grad_scores = (probs * (grad_probs - inner)).astype(BF16)
            grad_ref[i, :, cols] = (dot(grad_scores, keys, ((0,), (0,))) * SCALE).astype(BF16)
            grad_keys = dot(grad_scores, query, ((1,), (0,))) * SCALE
            grad_values = dot(probs.astype(BF16), grad, ((1,), (0,)))
            if i == blocks - 1:
                gk_ref[:keep, cols] = grad_keys
                gv_ref[:keep, cols] = grad_values
            else:
                gk_ref[:keep, cols] += grad_keys
                gv_ref[:keep, cols] += grad_values
    shape = (blocks, block_len, width)
    grad_ref[:, :, width : 2 * width] = gk_ref[...].reshape(shape).astype(BF16)
    grad_ref[:, :, 2 * width :] = gv_ref[...].reshape(shape).astype(BF16)


def local_call(kernel, outs, scratch, *operands):
    whole = pl.BlockSpec(memory_space=pltpu.VMEM)
    return pl.pallas_call(
        kernel,
        in_specs=[whole] * len(operands),
        out_specs=[whole] * len(outs),
        out_shape=outs,
        scratch_shapes=scratch,
        compiler_params=pltpu.CompilerParams(vmem_limit_bytes=48 * 1024 * 1024),
        cost_estimate=pl.CostEstimate(flops=4 * 10**9, bytes_accessed=8 * 10**6, transcendentals=0),
    )(*operands)


def shards(
    tokens,
    segments,
    ln1_gain,
    ln1_bias,
    qkv_weight,
    qkv_bias,
    out_weight,
    out_bias,
    ln2_gain,
    ln2_bias,
    fc_weight,
    fc_bias,
    proj_weight,
    proj_bias,
    grad_out,
):
    seq_count, shard_len, model_width = tokens.shape
    tp_count, ctx_count, dp_count = (lax.axis_size(n) for n in ("tp", "ctx", "dp"))
    tp_index, ctx_index, dp_index = (lax.axis_index(n) for n in ("tp", "ctx", "dp"))
    block_len = shard_len * tp_count
    key_len = block_len * ctx_count
    width_tp = qkv_weight.shape[2]
    piece = model_width // dp_count
    own_rows = seq_count * shard_len

    def turn(value, back=False):
        if dp_count == 1:
            return value
        start = dp_index * piece
        if back:
            start = lax.rem(model_width - start, model_width)
        return lax.dynamic_slice_in_dim(
            jnp.concatenate([value, value], axis=-1), start, model_width, value.ndim - 1
        )

    residual_in = turn(tokens.reshape(own_rows, model_width)).astype(F32)
    grad_low = turn(grad_out.reshape(own_rows, model_width))
    ln1_gain, ln1_bias, out_bias, ln2_gain, ln2_bias, proj_bias = [
        turn(v) for v in (ln1_gain, ln1_bias, out_bias, ln2_gain, ln2_bias, proj_bias)
    ]

    normed_one, scaled_one, inverse_one = normalize(residual_in, ln1_gain, ln1_bias)
    attn_rows = gathered(normed_one.astype(BF16), 0)
    qkv_flat = jnp.concatenate([qkv_weight[:, c] for c in range(3)], axis=1)
    qkv_full = turned(qkv_flat, "dp", 0)
    out_full = turned(out_weight, "dp", 1)
    fc_full = turned(fc_weight, "dp", 0)
    proj_full = turned(proj_weight, "dp", 1)
    grad_rows = turned(grad_low, "tp", 0)

    per_seq = ctx_count // seq_count
    group_width = width_tp // per_seq

    def by_group(rows, parts):
        rows = rows.reshape(tp_count, seq_count, shard_len, parts, per_seq, group_width)
        rows = rows.transpose(1, 4, 0, 2, 3, 5)
        return rows.reshape(ctx_count, block_len, parts * group_width)

    def by_rows(groups, parts):
        groups = groups.reshape(seq_count, per_seq, tp_count, shard_len, parts, group_width)
        groups = groups.transpose(2, 0, 3, 4, 1, 5)
        return groups.reshape(tp_count * own_rows, parts * width_tp)

    mixed = (dot(attn_rows, qkv_full, ((1,), (0,))) + qkv_bias.reshape(-1)).astype(BF16)
    mixed = exchange(swap_kernel, by_group(mixed, 3), "ctx", 2)

    within = jnp.arange(shard_len, dtype=jnp.int32)
    block_of = lax.rem(jnp.arange(tp_count, dtype=jnp.int32) + tp_index, tp_count)
    own_order = (block_of[:, None] * shard_len + within[None, :]).reshape(-1)
    places = jnp.arange(ctx_count, dtype=jnp.int32)[:, None] * block_len + own_order[None, :]
    document = lax.dynamic_index_in_dim(segments, ctx_index // per_seq, 0, False)
    document = document.reshape(ctx_count, tp_count, shard_len)
    document = lax.dynamic_slice_in_dim(
        jnp.concatenate([document, document], axis=1), tp_index, tp_count, 1
    ).reshape(ctx_count, block_len)
    places = (places, document, places.reshape(key_len, 1), document.reshape(key_len, 1))
    attended, log_totals = local_call(
        attend_kernel,
        [
            jax.ShapeDtypeStruct((ctx_count, block_len, group_width), BF16),
            jax.ShapeDtypeStruct((ctx_count * (group_width // HD), block_len), F32),
        ],
        [],
        mixed,
        *places,
    )
    attended_flat = by_rows(exchange(swap_kernel, attended, "ctx", 3), 1)
    branch = scattered_sum(dot(attended_flat, out_full, ((1,), (0,))), 1)
    middle = residual_in + branch + out_bias
    normed_two, scaled_two, inverse_two = normalize(middle, ln2_gain, ln2_bias)
    mlp_rows = gathered(normed_two.astype(BF16), 0)
    upward = dot(mlp_rows, fc_full, ((1,), (0,))) + fc_bias
    hidden, gelu_back = jax.vjp(gelu_tanh, upward)
    hidden_low = hidden.astype(BF16)

    grad_hidden = dot(grad_rows, proj_full, ((1,), (1,)))
    grad_up = gelu_back(grad_hidden)[0].astype(BF16)
    fc_bias_part = jnp.sum(grad_up, axis=0, dtype=F32)
    proj_weight_grad, proj_sent, proj_stages = weight_sum(
        dot(hidden_low, grad_rows, ((0,), (0,))), 1, 0
    )
    fc_weight_grad, fc_sent, fc_stages = weight_sum(dot(mlp_rows, grad_up, ((0,), (0,))), 0, 0)
    grad_normed_two = scattered_sum(dot(grad_up, fc_full, ((1,), (1,))), 4, proj_sent)
    mlp_out = turned_sum(dot(hidden_low, proj_full, ((1,), (0,))), "tp", 0)
    block_out = turn((middle + mlp_out + proj_bias).astype(BF16), True)

    grad_top = grad_low.astype(F32)
    grad_middle = grad_top + normalize_back(grad_normed_two, scaled_two, inverse_two, ln2_gain)
    middle_rows = gathered(grad_middle.astype(BF16), 5, [*fc_sent, *proj_stages[0]])
    grad_attended = by_group(dot(middle_rows, out_full, ((1,), (1,))).astype(BF16), 1)
    grad_attended = exchange(
        swap_kernel, grad_attended, "ctx", 6, [*fc_stages[0], *proj_stages[1]]
    )
    out_weight_grad, out_sent, out_stages = weight_sum(
        dot(attended_flat, middle_rows, ((0,), (0,))), 1, 0
    )

    (grad_groups,) = local_call(
        attend_back_kernel,
        [jax.ShapeDtypeStruct(mixed.shape, BF16)],
        [pltpu.VMEM((key_len, group_width), F32)] * 2,
        mixed,
        grad_attended,
        log_totals,
        *places,
    )
    grad_groups = exchange(
        swap_kernel, grad_groups, "ctx", 7, [*fc_stages[1], *proj_stages[2], *out_stages[0]]
    )
    grad_mixed = by_rows(grad_groups, 3)
    qkv_bias_part = jnp.sum(grad_mixed, axis=0, dtype=F32)
    qkv_grad, qkv_sent, _ = weight_sum(dot(attn_rows, grad_mixed, ((0,), (0,))), 0, 0)
    qkv_weight_grad = jnp.stack(jnp.split(qkv_grad, 3, axis=1), axis=1)
    grad_normed_one = scattered_sum(
        dot(grad_mixed, qkv_full, ((1,), (1,))),
        8,
        [*fc_stages[2], *proj_stages[3], *out_stages[1], *qkv_sent],
    )
    tokens_grad = grad_middle + normalize_back(grad_normed_one, scaled_one, inverse_one, ln1_gain)

    shared = jnp.stack(
        [
            jnp.sum(grad_normed_one * scaled_one, axis=0),
            jnp.sum(grad_normed_one, axis=0),
            jnp.sum(grad_middle, axis=0),
            jnp.sum(grad_normed_two * scaled_two, axis=0),
            jnp.sum(grad_normed_two, axis=0),
            jnp.sum(grad_top, axis=0),
        ]
    )
    shared = sum_small(turn(shared, True), ("dp", "ctx", "tp"))
    split_biases = sum_small(jnp.concatenate([qkv_bias_part, fc_bias_part]), ("dp", "ctx"))
    qkv_bias_grad = split_biases[: 3 * width_tp].reshape(3, width_tp)
    fc_bias_grad = split_biases[3 * width_tp :]
    ln1_gain_grad, ln1_bias_grad, out_bias_grad, ln2_gain_grad, ln2_bias_grad, proj_bias_grad = [
        shared[i] for i in range(6)
    ]
    return (
        block_out.reshape(tokens.shape),
        turn(tokens_grad, True).reshape(tokens.shape),
        ln1_gain_grad,
        ln1_bias_grad,
        qkv_weight_grad,
        qkv_bias_grad,
        out_weight_grad,
        out_bias_grad,
        ln2_gain_grad,
        ln2_bias_grad,
        fc_weight_grad,
        fc_bias_grad,
        proj_weight_grad,
        proj_bias_grad,
    )


def solution(mesh):
    placed = (
        P("dp", ("ctx", "tp"), None),
        P("dp", None),
        P(),
        P(),
        P("dp", None, "tp"),
        P(None, "tp"),
        P("tp", "dp"),
        P(),
        P(),
        P(),
        P("dp", "tp"),
        P("tp"),
        P("tp", "dp"),
        P(),
        P("dp", ("ctx", "tp"), None),
    )
    return jax.shard_map(
        shards,
        mesh=mesh,
        in_specs=placed,
        out_specs=(
            P("dp", ("ctx", "tp"), None),
            P("dp", ("ctx", "tp"), None),
            P(),
            P(),
            P("dp", None, "tp"),
            P(None, "tp"),
            P("tp", "dp"),
            P(),
            P(),
            P(),
            P("dp", "tp"),
            P("tp"),
            P("tp", "dp"),
            P(),
        ),
        check_vma=False,
    )
```
